32 devices in a mesh: wide: 8 (over z, y), narrow: 4 (over x, core).
Axes of the slice: x: 2, y: 2, z: 4, core: 2. Of those that a mesh axis runs over, the one named last changes fastest.
Arguments:
- velocity: float32 [3, 512, 4096], P(None, None, ('wide', 'narrow')), may hold values from -6 to 6
- element_slot: int32 [32, 128], P(('wide', 'narrow')), may hold values from 0 to 127, as said below
- corner_vertex: int32 [8, 4096], P(None, ('wide', 'narrow')), may hold values from 0 to 4351, as said below
- axial_size: float32 [8], P('wide'), may hold values from 0.5 to 2
- arc_size: float32 [16], replicated, may hold values from 0.5 to 2
- radial_size: float32 [16], replicated, may hold values from 0.3 to 1.5
- fdm_vectors: float32 [10, 10], replicated, may hold values from -2 to 2
- fdm_values: float32 [10], replicated, may hold values from 0.5 to 60
Outputs:
- velocity_out: float32 [3, 512, 4096], P(None, None, ('wide', 'narrow'))
- coarse_residual: float32 [3, 4352], P(None, ('wide', 'narrow'))
The draws below stay inside these ranges and needn't reach their ends.
Inputs may be any that keep to these rules, and one draw needn't show every extreme that they name: `element_slot`: each device's row is a permutation of the block positions of its 128 elements. `corner_vertex`: the ids of a permutation of the 4352 vertices of the coarse grid (vertex at axial index, around index and radial offset 0 to 16, periodic along and around the pipe); corner a * 4 + b * 2 + c lies at axial offset a, around offset b, radial offset c of its element; elements that share a corner share its id.
All inputs are finite; a program needn't handle non-finite values.
Results may differ from the reference program's by a relative error of at most 0.0001.
Values sent between devices are 32-bit elements; how exact they have to be, the bound alone decides.
A program may use at most 128 MiB of HBM per device.

```python
import math
from functools import partial
import jax
import jax.numpy as jnp
import numpy as np
from jax import lax

POINTS = 8
SPAN = 10
AXIAL_DEV = 1
AROUND_DEV = 8
RADIAL = 16
STEPS = 2
ELEMS_DEV = 128
AXIAL = 8
AROUND = 32
ELEMS = 4096
VERTICES = 4352
N_WIDE = 8
N_NARROW = 4


def layout_tables(key):
    wide_count = AXIAL // AXIAL_DEV
    narrow_count = AROUND // AROUND_DEV
    slot_keys = jax.random.split(jax.random.fold_in(key, 11), wide_count * narrow_count)
    slot_rows = jax.vmap(lambda sub_key: jax.random.permutation(sub_key, ELEMS_DEV))(slot_keys).astype(jnp.int32)
    relabel = jax.random.permutation(jax.random.fold_in(key, 12), VERTICES).astype(jnp.int32)
    return (slot_rows, relabel)


def draw_element_slot(key, part):
    return layout_tables(key)[0]


def draw_corner_vertex(key, part):
    slot_rows, relabel = layout_tables(key)
    narrow_count = AROUND // AROUND_DEV
    stored = jnp.arange(ELEMS, dtype=jnp.int32)
    device = stored // ELEMS_DEV
    position = slot_rows[device, stored % ELEMS_DEV]
    axial_index = device // narrow_count * AXIAL_DEV + position // (AROUND_DEV * RADIAL)
    around_index = device % narrow_count * AROUND_DEV + position // RADIAL % AROUND_DEV
    radial_index = position % RADIAL
    corners = []
    for corner in range(8):
        axial_spacing = corner // 4
        step_t = corner // 2 % 2
        step_r = corner % 2
        structured = ((axial_index + axial_spacing) % AXIAL * AROUND + (around_index + step_t) % AROUND) * (RADIAL + 1) + radial_index + step_r
        corners.append(relabel[structured])
    return jnp.stack(corners)


def block_scale(rng, dims, cuts, least, top_value):
    factor_of, own = 1.0, jax.random.fold_in(rng, 6)
    for dim, parts in cuts:
        steps = jnp.exp(jax.random.uniform(jax.random.fold_in(own, dim), (parts,), jnp.float32, least / len(cuts), top_value / len(cuts)))
        factor_of = factor_of * jnp.repeat(steps, dims[dim] // parts).reshape([-1 if axis == dim else 1 for axis in range(len(dims))])
    return factor_of


def noise(stream_key, shape, scale, reach, cuts=(), held_as=jnp.bfloat16):
    gain = block_scale(stream_key, shape, cuts, -0.22, 0.18) if cuts else 1.0
    values = jax.random.normal(stream_key, shape, jnp.float32) * scale * gain
    return jnp.minimum(jnp.maximum(values, -reach), reach).astype(held_as)


def setup_inputs(seed: int = 0) -> dict:
    seeds = jax.random.split(jax.random.key(seed), 9)
    return {
        "velocity": noise(seeds[0], (3, POINTS * POINTS * POINTS, ELEMS), 1.0, 6.0, ((2, 32),), jnp.float32),
        "element_slot": draw_element_slot(jax.random.fold_in(seeds[8], 71), 0),
        "corner_vertex": draw_corner_vertex(jax.random.fold_in(seeds[8], 71), 0),
        "axial_size": jnp.clip(jnp.exp(math.log(2.0) - 1.3862944 * jax.random.uniform(seeds[3], (AXIAL,), jnp.float32) ** block_scale(seeds[3], (AXIAL,), ((0, 8),), -0.2, 0.2)), 0.5, 2.0),
        "arc_size": jnp.clip(jnp.exp(jax.random.uniform(seeds[4], (RADIAL,), jnp.float32, math.log(0.5), math.log(2.0))), 0.5, 2.0),
        "radial_size": jnp.clip(jnp.exp(jax.random.uniform(seeds[5], (RADIAL,), jnp.float32, math.log(0.3), math.log(1.5))), 0.3, 1.5),
        "fdm_vectors": noise(seeds[6], (SPAN, SPAN), SPAN ** -0.5, 2.0, (), jnp.float32),
        "fdm_values": jnp.clip(jnp.exp(jax.random.uniform(seeds[7], (SPAN,), jnp.float32, math.log(0.5), math.log(60.0))), 0.5, 60.0),
    }


SIGMA = 4.0
VISCOSITY = 0.05
HIGH_ACCURACY = lax.Precision.HIGHEST


def node_tables():
    gll_nodes = np.array([-1.0, -0.8717401485096066, -0.5917001814331423, -0.2092992179024789, 0.2092992179024789, 0.5917001814331423, 0.8717401485096066, 1.0])
    gll_weights = np.array([1.0 / 28.0, 0.2107042271435061, 0.3411226924835044, 0.4124587946587038, 0.4124587946587038, 0.3411226924835044, 0.2107042271435061, 1.0 / 28.0])
    bary_scale = np.array([np.prod([gll_nodes[target] - gll_nodes[partner] for partner in range(8) if partner != target]) for target in range(8)])
    derivative = np.zeros((8, 8))
    for target in range(8):
        for source in range(8):
            if target != source:
                derivative[target, source] = bary_scale[target] / (bary_scale[source] * (gll_nodes[target] - gll_nodes[source]))
        derivative[target, target] = -np.sum(derivative[target])
    fine_nodes = np.array([-0.9815606342467192, -0.9041172563704749, -0.7699026741943047, -0.5873179542866175, -0.3678314989981802, -0.1252334085114689, 0.1252334085114689, 0.3678314989981802, 0.5873179542866175, 0.7699026741943047, 0.9041172563704749, 0.9815606342467192])
    fine_weights = np.array([0.0471753363865118, 0.1069393259953184, 0.1600783285433462, 0.2031674267230659, 0.2334925365383548, 0.2491470458134028, 0.2491470458134028, 0.2334925365383548, 0.2031674267230659, 0.1600783285433462, 0.1069393259953184, 0.0471753363865118])
    interp = np.ones((12, 8))
    for source in range(8):
        for partner in range(8):
            if partner != source:
                interp[:, source] = interp[:, source] * (fine_nodes - gll_nodes[partner]) / (gll_nodes[source] - gll_nodes[partner])
    linear = np.stack([(1.0 - gll_nodes) / 2.0, (1.0 + gll_nodes) / 2.0])
    corner_map = (linear[:, None, None, :, None, None] * linear[None, :, None, None, :, None] * linear[None, None, :, None, None, :]).reshape(8, 512)
    mass_gll = gll_weights[:, None, None] * gll_weights[None, :, None] * gll_weights[None, None, :]
    mass_fine = fine_weights[:, None, None] * fine_weights[None, :, None] * fine_weights[None, None, :]
    return tuple(jnp.asarray(matrix, jnp.float32) for matrix in (derivative, interp, corner_map, mass_gll, mass_fine))


def apply_first(matrix, tensor):
    return jnp.einsum('ai,cijkb->cajkb', matrix, tensor, precision=HIGH_ACCURACY)


def apply_second(matrix, tensor):
    return jnp.einsum('aj,cijkb->ciakb', matrix, tensor, precision=HIGH_ACCURACY)


def apply_third(matrix, tensor):
    return jnp.einsum('ak,cijkb->cijab', matrix, tensor, precision=HIGH_ACCURACY)


def to_fine(tensor, interp):
    return apply_third(interp, apply_second(interp, apply_first(interp, tensor)))


def to_gll(tensor, interp):
    return apply_third(interp.T, apply_second(interp.T, apply_first(interp.T, tensor)))


def element_residual(velocity, lengths, tables):
    derivative, interp, corner_map, mass_gll, mass_fine = tables
    block_width = velocity.shape[-1]
    tensor = velocity.reshape(3, 8, 8, 8, block_width)
    inverse = 2.0 / lengths
    volume = lengths[0] * lengths[1] * lengths[2] / 8.0
    grad_z = apply_first(derivative, tensor) * inverse[0]
    grad_t = apply_second(derivative, tensor) * inverse[1]
    grad_r = apply_third(derivative, tensor) * inverse[2]
    fine_vel = to_fine(tensor, interp)
    convective_term = fine_vel[0:1] * to_fine(grad_z, interp) + fine_vel[1:2] * to_fine(grad_t, interp) + fine_vel[2:3] * to_fine(grad_r, interp)
    convective_term = convective_term * (mass_fine[:, :, :, None] * volume)
    advect_velocity = to_gll(convective_term, interp)
    weight = mass_gll[:, :, :, None] * volume
    stiff = apply_first(derivative.T, grad_z * weight) * inverse[0]
    stiff = stiff + apply_second(derivative.T, grad_t * weight) * inverse[1]
    stiff = stiff + apply_third(derivative.T, grad_r * weight) * inverse[2]
    return -(advect_velocity + VISCOSITY * stiff).reshape(3, 512, block_width)


def quadratic_form(direction, lengths, tables):
    derivative = tables[0]
    mass_gll = tables[3]
    block_width = direction.shape[-1]
    tensor = direction.reshape(3, 8, 8, 8, block_width)
    inverse = 2.0 / lengths
    volume = lengths[0] * lengths[1] * lengths[2] / 8.0
    weight = mass_gll[:, :, :, None] * volume
    grad_z = apply_first(derivative, tensor) * inverse[0]
    grad_t = apply_second(derivative, tensor) * inverse[1]
    grad_r = apply_third(derivative, tensor) * inverse[2]
    return jnp.sum(weight * (SIGMA * tensor * tensor + VISCOSITY * (grad_z * grad_z + grad_t * grad_t + grad_r * grad_r)))


def fdm_solve(extended, lengths, vectors, values):
    block_width = extended.shape[-1]
    tensor = extended.reshape(3, 10, 10, 10, block_width)
    spectral = apply_third(vectors.T, apply_second(vectors.T, apply_first(vectors.T, tensor)))
    squared = (2.0 / lengths) ** 2
    volume = lengths[0] * lengths[1] * lengths[2] / 8.0
    scaling = volume * (SIGMA + VISCOSITY * (values[:, None, None, None] * squared[0] + values[None, :, None, None] * squared[1] + values[None, None, :, None] * squared[2]))
    spectral = spectral / scaling
    restored = apply_third(vectors, apply_second(vectors, apply_first(vectors, spectral)))
    return restored[:, 1:9, 1:9, 1:9].reshape(3, 512, block_width)


def blockwise(function, arrays, block_width):
    blocks_total = arrays[0].shape[-1] // block_width

    def single(block_index):
        pieces = [lax.dynamic_slice_in_dim(member, block_index * block_width, block_width, member.ndim - 1) for member in arrays]
        return function(*pieces)

    stacked = lax.map(single, jnp.arange(blocks_total, dtype=jnp.int32))
    if stacked.ndim == 1:
        return jnp.sum(stacked)
    reordered = jnp.moveaxis(stacked, 0, -2)
    return reordered.reshape(reordered.shape[:-2] + (blocks_total * block_width,))


def node_masks(elem_count):
    node_index = jnp.arange(512)
    node_i = node_index // 64
    node_j = (node_index // 8) % 8
    node_k = node_index % 8
    radial_pos = jnp.arange(elem_count) % RADIAL
    on_wall = ((node_k == 0)[:, None] & (radial_pos == 0)[None]) | ((node_k == 7)[:, None] & (radial_pos == RADIAL - 1)[None])
    wall_keep = jnp.where(on_wall, 0.0, 1.0).astype(jnp.float32)
    face_z = jnp.where((node_i == 0) | (node_i == 7), 2.0, 1.0)[:, None]
    face_t = jnp.where((node_j == 0) | (node_j == 7), 2.0, 1.0)[:, None]
    inner_r = ((node_k == 0)[:, None] & (radial_pos > 0)[None]) | ((node_k == 7)[:, None] & (radial_pos < RADIAL - 1)[None])
    sharing = (face_z * face_t * jnp.where(inner_r, 2.0, 1.0)).astype(jnp.float32)
    return wall_keep, sharing


def take_part(tensor, axis_pos, start, stop):
    return lax.slice_in_dim(tensor, start, stop, axis=axis_pos)


def shifted(tensor, elem_axis, offset, periodic):
    if periodic:
        return jnp.roll(tensor, offset, axis=elem_axis)
    elem_count = tensor.shape[elem_axis]
    zero_part = jnp.zeros_like(take_part(tensor, elem_axis, 0, 1))
    if offset > 0:
        return jnp.concatenate([zero_part, take_part(tensor, elem_axis, 0, elem_count - 1)], axis=elem_axis)
    return jnp.concatenate([take_part(tensor, elem_axis, 1, elem_count), zero_part], axis=elem_axis)


def shared_sum(tensor, node_axis, elem_axis, periodic):
    low_plane = take_part(tensor, node_axis, 0, 1)
    high_plane = take_part(tensor, node_axis, 7, 8)
    next_low = shifted(low_plane, elem_axis, -1, periodic)
    previous_upper_plane = shifted(high_plane, elem_axis, 1, periodic)
    middle = take_part(tensor, node_axis, 1, 7)
    return jnp.concatenate([low_plane + previous_upper_plane, middle, high_plane + next_low], axis=node_axis)


def widened(tensor, node_axis, elem_axis, periodic):
    lower = shifted(take_part(tensor, node_axis, 6, 7), elem_axis, 1, periodic)
    upper = shifted(take_part(tensor, node_axis, 1, 2), elem_axis, -1, periodic)
    return jnp.concatenate([lower, tensor, upper], axis=node_axis)


def reference(velocity, element_slot, corner_vertex, axial_size, arc_size, radial_size, fdm_vectors, fdm_values):
    tables = node_tables()
    devices = N_WIDE * N_NARROW
    block_width = min(128, ELEMS_DEV)
    inverse_slot = jnp.zeros((devices, ELEMS_DEV), jnp.int32).at[jnp.arange(devices)[:, None], element_slot].set(
        jnp.broadcast_to(jnp.arange(ELEMS_DEV, dtype=jnp.int32)[None], (devices, ELEMS_DEV)))

    def to_struct(tensor):
        channels = tensor.shape[0]
        grouped = tensor.reshape(channels, -1, devices, ELEMS_DEV)
        placed = jnp.take_along_axis(grouped, inverse_slot[None, None], axis=3)
        placed = placed.reshape(channels, -1, N_WIDE, N_NARROW, AXIAL_DEV, AROUND_DEV, RADIAL)
        placed = placed.transpose(0, 1, 2, 4, 3, 5, 6)
        return placed.reshape(channels, -1, ELEMS)

    def from_struct(tensor):
        channels = tensor.shape[0]
        placed = tensor.reshape(channels, -1, N_WIDE, AXIAL_DEV, N_NARROW, AROUND_DEV, RADIAL)
        placed = placed.transpose(0, 1, 2, 4, 3, 5, 6).reshape(channels, -1, devices, ELEMS_DEV)
        stored = jnp.take_along_axis(placed, element_slot[None, None], axis=3)
        return stored.reshape(channels, -1, ELEMS)

    def assemble(tensor):
        channels = tensor.shape[0]
        grid_view = tensor.reshape(channels, 8, 8, 8, AXIAL, AROUND, RADIAL)
        grid_view = shared_sum(grid_view, 1, 4, True)
        grid_view = shared_sum(grid_view, 2, 5, True)
        grid_view = shared_sum(grid_view, 3, 6, False)
        return grid_view.reshape(tensor.shape)

    def widen(tensor):
        grid_view = tensor.reshape(3, 8, 8, 8, AXIAL, AROUND, RADIAL)
        grid_view = widened(grid_view, 1, 4, True)
        grid_view = widened(grid_view, 2, 5, True)
        grid_view = widened(grid_view, 3, 6, False)
        return grid_view.reshape(3, 1000, ELEMS)

    shape_grid = (AXIAL, AROUND, RADIAL)
    axial_len = jnp.broadcast_to(axial_size[:, None, None], shape_grid)
    around_len = jnp.broadcast_to(arc_size[None, None, :], shape_grid)
    radial_len = jnp.broadcast_to(radial_size[None, None, :], shape_grid)
    lengths = jnp.stack([axial_len, around_len, radial_len]).reshape(3, ELEMS)
    volume = lengths[0] * lengths[1] * lengths[2] / 8.0
    node_mass = tables[3].reshape(512)[:, None] * volume[None]
    wall_keep, sharing = node_masks(ELEMS)

    stored_first = to_struct(velocity)
    summed = assemble(jnp.concatenate([stored_first * node_mass[None], node_mass[None]], 0))
    velocity_now = summed[:3] / summed[3:4] * wall_keep
    residual_fn = partial(element_residual, tables=tables)
    solve_fn = partial(fdm_solve, vectors=fdm_vectors, values=fdm_values)
    quad_fn = partial(quadratic_form, tables=tables)
    for step_index in range(STEPS):
        local_res = blockwise(residual_fn, (velocity_now, lengths), block_width) * wall_keep
        assembled = assemble(local_res)
        extended = widen(assembled)
        correction = blockwise(solve_fn, (extended, lengths), block_width)
        direction = assemble(correction / sharing) * wall_keep
        numerator = jnp.sum(assembled * direction / sharing)
        denominator = blockwise(quad_fn, (direction, lengths), block_width)
        velocity_now = velocity_now + (numerator / denominator) * direction
    final_res = blockwise(residual_fn, (velocity_now, lengths), block_width) * wall_keep
    corner_sums = jnp.einsum('qp,cpe->cqe', tables[2], final_res, precision=HIGH_ACCURACY)
    vertex_ids = to_struct(corner_vertex[None]).reshape(-1)
    coarse = jax.ops.segment_sum(corner_sums.reshape(3, -1).T, vertex_ids, num_segments=VERTICES).T
    return from_struct(velocity_now), coarse
```

```python
from functools import partial

import jax
import jax.numpy as jnp
import ml_dtypes
import numpy as np
from jax import lax
from jax.experimental import pallas as pl
from jax.experimental.pallas import tpu as pltpu
from jax.sharding import PartitionSpec as P

AROUND_DEV = 8
RADIAL = 16
STEPS = 2
SIGMA = 4.0
VISCOSITY = 0.05
LIMIT = 48 * 1024 * 1024
MESH = pl.DeviceIdType.MESH
F32 = jnp.float32
BF16 = jnp.bfloat16


def node_tables():
    gll_nodes = np.array(
        [
            -1.0,
            -0.8717401485096066,
            -0.5917001814331423,
            -0.2092992179024789,
            0.2092992179024789,
            0.5917001814331423,
            0.8717401485096066,
            1.0,
        ]
    )
    gll_weights = np.array(
        [
            1.0 / 28.0,
            0.2107042271435061,
            0.3411226924835044,
            0.4124587946587038,
            0.4124587946587038,
            0.3411226924835044,
            0.2107042271435061,
            1.0 / 28.0,
        ]
    )
    bary_scale = np.array(
        [
            np.prod(
                [
                    gll_nodes[target] - gll_nodes[partner]
                    for partner in range(8)
                    if partner != target
                ]
            )
            for target in range(8)
        ]
    )
    derivative = np.zeros((8, 8))
    for target in range(8):
        for source in range(8):
            if target != source:
                derivative[target, source] = bary_scale[target] / (
                    bary_scale[source] * (gll_nodes[target] - gll_nodes[source])
                )
        derivative[target, target] = -np.sum(derivative[target])
    fine_nodes = np.array(
        [
            -0.9815606342467192,
            -0.9041172563704749,
            -0.7699026741943047,
            -0.5873179542866175,
            -0.3678314989981802,
            -0.1252334085114689,
            0.1252334085114689,
            0.3678314989981802,
            0.5873179542866175,
            0.7699026741943047,
            0.9041172563704749,
            0.9815606342467192,
        ]
    )
    fine_weights = np.array(
        [
            0.0471753363865118,
            0.1069393259953184,
            0.1600783285433462,
            0.2031674267230659,
            0.2334925365383548,
            0.2491470458134028,
            0.2491470458134028,
            0.2334925365383548,
            0.2031674267230659,
            0.1600783285433462,
            0.1069393259953184,
            0.0471753363865118,
        ]
    )
    interp = np.ones((12, 8))
    for source in range(8):
        for partner in range(8):
            if partner != source:
                interp[:, source] = (
                    interp[:, source]
                    * (fine_nodes - gll_nodes[partner])
                    / (gll_nodes[source] - gll_nodes[partner])
                )
    linear = np.stack([(1.0 - gll_nodes) / 2.0, (1.0 + gll_nodes) / 2.0])
    corner_map = (
        linear[:, None, None, :, None, None]
        * linear[None, :, None, None, :, None]
        * linear[None, None, :, None, None, :]
    ).reshape(8, 512)
    mass_gll = gll_weights[:, None, None] * gll_weights[None, :, None] * gll_weights[None, None, :]
    mass_fine = (
        fine_weights[:, None, None] * fine_weights[None, :, None] * fine_weights[None, None, :]
    )
    dealias_interp_matrix = np.kron(interp, np.kron(interp, interp))
    return derivative, interp, corner_map, gll_weights, fine_weights


def stack_const(matrix):
    high = matrix.astype(ml_dtypes.bfloat16)
    low = (matrix - high.astype(np.float64)).astype(ml_dtypes.bfloat16)
    return np.concatenate([high, low, high], axis=1)


DERIV, INTERP, CORNER, WGLL, WFINE = node_tables()
INTERP_DERIV = INTERP @ DERIV
BEND = DERIV.T @ np.diag(WGLL) @ DERIV
FORWARD = stack_const(
    np.concatenate(
        [np.kron(INTERP, INTERP), np.kron(INTERP_DERIV, INTERP), np.kron(INTERP, INTERP_DERIV)]
    )
)
BACKWARD = stack_const((np.kron(INTERP, INTERP) * np.kron(WFINE, WFINE)[:, None]).T)
STIFF = stack_const(
    np.concatenate([np.kron(BEND, np.diag(WGLL)), np.kron(np.diag(WGLL), BEND)])
)
WEIGHT_JK = np.kron(WGLL, WGLL).astype(np.float32)


def split_rows(x):
    high = x.astype(BF16)
    low = (x - high.astype(F32)).astype(BF16)
    return jnp.concatenate([high, high, low], axis=0)


def split_cols(x):
    high = x.astype(BF16)
    low = (x - high.astype(F32)).astype(BF16)
    return jnp.concatenate([high, low, high], axis=1)


def mm(a, b):
    return jnp.dot(a, b, preferred_element_type=F32)


def combine(coefs, planes):
    total = None
    for coef, plane in zip(coefs, planes):
        term = plane * coef
        total = term if total is None else total + term
    return total


def lane_roll(x, shift):
    parts = [
        pltpu.roll(x[:, b : b + 128], shift, 1) for b in range(0, x.shape[1], 128)
    ]
    return jnp.concatenate(parts, axis=1)


def row_k(shape):
    return lax.broadcasted_iota(jnp.int32, shape, 0) % 8


def keep_mask(shape, low_in, high_in):
    k = row_k(shape)
    return jnp.where(k == 0, low_in, 1.0) * jnp.where(k == 7, high_in, 1.0)


def inverse_mult(shape, low_in, high_in, plane):
    k = row_k(shape)
    j = lax.broadcasted_iota(jnp.int32, shape, 0) // 8
    scale = jnp.where((j == 0) | (j == 7), 0.5, 1.0)
    scale = scale * jnp.where(k == 0, 1.0 - 0.5 * low_in, 1.0)
    scale = scale * jnp.where(k == 7, 1.0 - 0.5 * high_in, 1.0)
    return scale * 0.5 if plane in (0, 7) else scale


def around(mine, other, up):
    lane = lax.broadcasted_iota(jnp.int32, mine.shape, 1) % 128
    if up:
        return lane_roll(jnp.where(lane >= 128 - RADIAL, other, mine), RADIAL)
    return lane_roll(jnp.where(lane < RADIAL, other, mine), 128 - RADIAL)


def radial_sum(x, low_in, high_in):
    rows = x.shape[0]
    k = row_k(x.shape)
    below = lane_roll(pltpu.roll(x, rows - 7, 0), 1)
    above = lane_roll(pltpu.roll(x, 7, 0), 127)
    return x + jnp.where(k == 0, below * low_in, 0.0) + jnp.where(k == 7, above * high_in, 0.0)


def around_sum(y, prev_high, next_low):
    low = y[0:8] + around(y[56:64], prev_high, True)
    high = y[56:64] + around(y[0:8], next_low, False)
    return low, high


def stiffness(planes, index, geo, stiff, weight_jk):
    mixed = mm(stiff, split_rows(planes[index]))
    along = combine([float(v) for v in BEND[index]], planes) * weight_jk
    inv0, inv1, inv2 = geo[0:1], geo[1:2], geo[2:3]
    across = mixed[0:64] * (inv1 * inv1) + mixed[64:128] * (inv2 * inv2)
    return along * (inv0 * inv0) + across * float(WGLL[index])


def write_residual(u, geo, fwd_ref, back_ref, stiff_ref, wjk, out_ref, fine_ref):
    inv = [geo[d : d + 1, 0:128] for d in range(3)]
    volume, low_in, high_in = geo[3:4], geo[4:5], geo[5:6]
    fwd = fwd_ref[...]
    back = back_ref[...]
    stiff = stiff_ref[...]
    planes = [u[i] for i in range(8)]
    for a in range(12):
        plain = combine([float(v) for v in INTERP[a]], planes)
        slope = combine([float(v) for v in INTERP_DERIV[a]], planes)
        fine = mm(fwd, split_rows(plain))
        along = mm(fwd[0:144], split_rows(slope))
        speed = [fine[0:144, 128 * d : 128 * d + 128] * inv[d] for d in range(3)]
        terms = []
        for c in range(3):
            lanes = slice(128 * c, 128 * c + 128)
            terms.append(
                speed[0] * along[:, lanes]
                + speed[1] * fine[144:288, lanes]
                + speed[2] * fine[288:432, lanes]
            )
        fine_ref[a] = mm(back, split_rows(jnp.concatenate(terms, axis=1)))
    keep = keep_mask((64, 384), low_in, high_in)
    for i in range(8):
        advect = combine(
            [float(v) for v in INTERP[:, i] * WFINE], [fine_ref[a] for a in range(12)]
        )
        bend = stiffness(planes, i, geo, stiff, wjk)
        out_ref[i] = -(advect + VISCOSITY * bend) * volume * keep


def first_kernel(y_ref, prev_ref, next_ref, geo_ref, fwd, back, stiff, wjk_ref, u_ref, res_ref, fine_ref):
    geo = geo_ref[...]
    low4 = jnp.concatenate([geo[4:5], geo[4:5, 0:128]], axis=1)
    high4 = jnp.concatenate([geo[5:6], geo[5:6, 0:128]], axis=1)
    keep = keep_mask((64, 384), geo[4:5], geo[5:6])
    for i in range(8):
        y = y_ref[i]
        low, high = around_sum(y, prev_ref[i], next_ref[i])
        total = radial_sum(jnp.concatenate([low, y[8:56], high], axis=0), low4, high4)
        mass = total[:, 384:512]
        u_ref[i] = total[:, 0:384] / jnp.concatenate([mass, mass, mass], axis=1) * keep
    write_residual(u_ref, geo, fwd, back, stiff, wjk_ref[...], res_ref, fine_ref)


def next_kernel(u_in, dirn_ref, sums_ref, geo_ref, fwd, back, stiff, wjk_ref, u_ref, res_ref, fine_ref):
    sums = sums_ref[...]
    step = jnp.sum(sums[0:1], axis=1, keepdims=True) / jnp.sum(sums[1:2], axis=1, keepdims=True)
    for i in range(8):
        u_ref[i] = u_in[i] + dirn_ref[i] * step
    write_residual(u_ref, geo_ref[...], fwd, back, stiff, wjk_ref[...], res_ref, fine_ref)


def solve_kernel(y_ref, prev_ref, next_ref, geo_ref, s_ref, lam_ref, into_ref, back_ref, lam2_ref, res_ref, corr_ref, ext_ref, spec_ref):
    geo = geo_ref[...]
    volume, low_in, high_in = geo[3:4], geo[4:5], geo[5:6]
    into = split_cols(into_ref[...])
    back = split_cols(back_ref[...])
    for i in range(10):
        y = y_ref[i]
        prev, following = prev_ref[i], next_ref[i]
        low, high = around_sum(y, prev[8:16], following[0:8])
        outer_low = around(y[48:56], prev[0:8], True)
        outer_high = around(y[8:16], following[8:16], False)
        wide = jnp.concatenate([outer_low, low, y[8:56], high, outer_high], axis=0)
        wide = radial_sum(wide, low_in, high_in)
        if 1 <= i <= 8:
            res_ref[i - 1] = wide[8:72]
        k = row_k(wide.shape)
        halo = jnp.where(k == 6, lane_roll(wide, 1) * low_in, 0.0)
        halo = jnp.where(k == 1, lane_roll(wide, 127) * high_in, halo)
        ext_ref[i] = mm(into, split_rows(jnp.concatenate([wide, halo], axis=0)))
    sq = [geo[d : d + 1] * geo[d : d + 1] for d in range(3)]
    lam2 = lam2_ref[...]
    cross = (lam2[:, 0:1] * sq[1] + lam2[:, 1:2] * sq[2]) * VISCOSITY + SIGMA
    for a in range(10):
        spectral = combine([s_ref[i, a] for i in range(10)], [ext_ref[i] for i in range(10)])
        scaling = volume * (cross + (VISCOSITY * lam_ref[a]) * sq[0])
        spec_ref[a] = mm(back, split_rows(spectral / scaling))
    for i in range(8):
        corr = combine([s_ref[i + 1, a] for a in range(10)], [spec_ref[a] for a in range(10)])
        corr_ref[i] = corr * inverse_mult((64, 384), low_in, high_in, i)


def direction_kernel(y_ref, prev_ref, next_ref, res_ref, geo_ref, stiff_ref, wjk_ref, dirn_ref, sums_ref):
    geo = geo_ref[...]
    volume, low_in, high_in = geo[3:4], geo[4:5], geo[5:6]
    wjk = wjk_ref[...]
    stiff = stiff_ref[...]
    keep = keep_mask((64, 384), low_in, high_in)
    numer = jnp.zeros((64, 384), F32)
    for i in range(8):
        y = y_ref[i]
        low, high = around_sum(y, prev_ref[i], next_ref[i])
        total = radial_sum(jnp.concatenate([low, y[8:56], high], axis=0), low_in, high_in)
        total = total * keep
        dirn_ref[i] = total
        numer = numer + res_ref[i] * total * inverse_mult((64, 384), low_in, high_in, i)
    planes = [dirn_ref[i] for i in range(8)]
    denom = jnp.zeros((64, 384), F32)
    for i in range(8):
        bend = stiffness(planes, i, geo, stiff, wjk)
        mass = wjk * float(SIGMA * WGLL[i])
        denom = denom + planes[i] * (mass * planes[i] + VISCOSITY * bend)
    denom = denom * volume

    def fold(x):
        x = jnp.sum(x, axis=0, keepdims=True)
        return x[:, 0:128] + x[:, 128:256] + x[:, 256:384]

    row = lax.broadcasted_iota(jnp.int32, (8, 128), 0)
    sums_ref[...] = jnp.where(row == 0, fold(numer), jnp.where(row == 1, fold(denom), 0.0))


def sum_kernel(wide, narrow, scatter, x_ref, o_ref, from_narrow, part, from_wide, s1, r1, s2, r2):
    w, n = lax.axis_index("wide"), lax.axis_index("narrow")
    barrier = pltpu.get_barrier_semaphore()
    for k in range(1, narrow):
        pl.semaphore_signal(barrier, inc=1, device_id=(w, (n + k) % narrow), device_id_type=MESH)
    for k in range(1, wide):
        pl.semaphore_signal(barrier, inc=1, device_id=((w + k) % wide, n), device_id_type=MESH)
    pl.semaphore_wait(barrier, narrow + wide - 2)
    copies = []
    for k in range(1, narrow):
        peer = (n + k) % narrow
        copy = pltpu.make_async_remote_copy(
            src_ref=x_ref.at[peer] if scatter else x_ref,
            dst_ref=from_narrow.at[k - 1],
            send_sem=s1.at[k - 1],
            recv_sem=r1.at[k - 1],
            device_id=(w, peer),
            device_id_type=MESH,
        )
        copy.start()
        copies.append(copy)
    total = x_ref[n] if scatter else x_ref[...]
    for k, copy in enumerate(copies):
        copy.wait()
        total = total + from_narrow[k]
    part[...] = total
    copies = []
    for k in range(1, wide):
        peer = (w + k) % wide
        copy = pltpu.make_async_remote_copy(
            src_ref=part.at[peer] if scatter else part,
            dst_ref=from_wide.at[k - 1],
            send_sem=s2.at[k - 1],
            recv_sem=r2.at[k - 1],
            device_id=(peer, n),
            device_id_type=MESH,
        )
        copy.start()
        copies.append(copy)
    total = part[w] if scatter else part[...]
    for k, copy in enumerate(copies):
        copy.wait()
        total = total + from_wide[k]
    o_ref[...] = total


def device_sum(x, scatter, ident):
    wide, narrow = lax.axis_size("wide"), lax.axis_size("narrow")
    middle = x.shape[1:] if scatter else x.shape
    last = middle[1:] if scatter else x.shape
    return pl.pallas_call(
        partial(sum_kernel, wide, narrow, scatter),
        out_shape=jax.ShapeDtypeStruct(last, F32),
        in_specs=[pl.BlockSpec(memory_space=pltpu.VMEM)],
        out_specs=pl.BlockSpec(memory_space=pltpu.VMEM),
        scratch_shapes=[
            pltpu.VMEM((narrow - 1,) + middle, F32),
            pltpu.VMEM(middle, F32),
            pltpu.VMEM((wide - 1,) + last, F32),
            pltpu.SemaphoreType.DMA((narrow - 1,)),
            pltpu.SemaphoreType.DMA((narrow - 1,)),
            pltpu.SemaphoreType.DMA((wide - 1,)),
            pltpu.SemaphoreType.DMA((wide - 1,)),
        ],
        compiler_params=pltpu.CompilerParams(
            collective_id=ident, has_side_effects=True, vmem_limit_bytes=LIMIT
        ),
    )(x)


def local_call(body, args, outs, scratch, smem=()):
    return pl.pallas_call(
        body,
        out_shape=[jax.ShapeDtypeStruct(s, F32) for s in outs],
        in_specs=[
            pl.BlockSpec(memory_space=pltpu.SMEM if p in smem else pltpu.VMEM)
            for p in range(len(args))
        ],
        out_specs=[pl.BlockSpec(memory_space=pltpu.VMEM)] * len(outs),
        scratch_shapes=[pltpu.VMEM(s, F32) for s in scratch],
        compiler_params=pltpu.CompilerParams(vmem_limit_bytes=LIMIT),
    )(*args)


def swap(axis, to_prev, to_next):
    count = lax.axis_size(axis)
    from_prev = lax.ppermute(to_next, axis, [(i, (i + 1) % count) for i in range(count)])
    from_next = lax.ppermute(to_prev, axis, [((i + 1) % count, i) for i in range(count)])
    return from_prev, from_next


def exchange(x):
    below, above = swap("wide", x[0:1], x[7:8])
    y = jnp.concatenate([x[0:1] + below, x[1:7], x[7:8] + above], axis=0)
    prev, following = swap("narrow", y[:, 0:8], y[:, 56:64])
    return y, prev, following


def exchange_wide(x):
    below, above = swap("wide", x[0:2], x[6:8])
    y = jnp.concatenate(
        [below[0:1], x[0:1] + below[1:2], x[1:7], x[7:8] + above[0:1], above[1:2]], axis=0
    )
    prev, following = swap("narrow", y[:, 0:16], y[:, 48:64])
    return y, prev, following


def shards(
    velocity,
    element_slot,
    corner_vertex,
    axial_size,
    arc_size,
    radial_size,
    fdm_vectors,
    fdm_values,
):
    wide_count, narrow_count = lax.axis_size("wide"), lax.axis_size("narrow")
    slot_of = element_slot[0]
    inverse_slot = jnp.zeros((128,), jnp.int32).at[slot_of].set(jnp.arange(128, dtype=jnp.int32))
    er = jnp.arange(128) % RADIAL
    hz = jnp.broadcast_to(axial_size, (128,))
    ht = jnp.tile(arc_size, AROUND_DEV)
    hr = jnp.tile(radial_size, AROUND_DEV)
    volume = hz * ht * hr / 8.0
    zero = jnp.zeros((128,), F32)
    rows = [2.0 / hz, 2.0 / ht, 2.0 / hr, volume]
    rows += [jnp.where(er > 0, 1.0, 0.0), jnp.where(er < RADIAL - 1, 1.0, 0.0), zero, zero]
    geo = jnp.tile(jnp.stack(rows).astype(F32), (1, 3))
    fwd, back, stiff = jnp.asarray(FORWARD), jnp.asarray(BACKWARD), jnp.asarray(STIFF)
    wjk = jnp.broadcast_to(jnp.asarray(WEIGHT_JK)[:, None], (64, 384))
    consts = (geo, fwd, back, stiff, wjk)

    transform = fdm_vectors.T.reshape(10, 1, 10, 1) * fdm_vectors.T.reshape(1, 10, 1, 10)
    own = transform[..., 1:9].reshape(100, 80)
    halo = jnp.zeros((10, 10, 10, 8), F32)
    halo = halo.at[..., 6].set(transform[..., 0]).at[..., 1].set(transform[..., 9])
    into = jnp.pad(jnp.concatenate([own, halo.reshape(100, 80)], axis=1), ((0, 12), (0, 0)))
    inner = fdm_vectors[1:9]
    outof = (inner.reshape(8, 1, 10, 1) * inner.reshape(1, 8, 1, 10)).reshape(64, 100)
    outof = jnp.pad(outof, ((0, 0), (0, 12)))
    lam2 = jnp.stack([jnp.repeat(fdm_values, 10), jnp.tile(fdm_values, 10)], axis=1)
    lam2 = jnp.pad(lam2, ((0, 12), (0, 126)), constant_values=1.0)

    mass = (np.kron(WGLL, np.kron(WGLL, WGLL)).astype(np.float32))[:, None] * volume[None]
    stored = velocity[:, :, inverse_slot] * mass[None]
    field = jnp.concatenate([stored[0], stored[1], stored[2], mass], axis=1).reshape(8, 64, 512)

    shape = (8, 64, 384)
    u, res = local_call(first_kernel, exchange(field) + consts, [shape, shape], [(12, 64, 384)])
    for step in range(STEPS):
        total, corr = local_call(
            solve_kernel,
            exchange_wide(res) + (geo, fdm_vectors, fdm_values, into, outof, lam2),
            [shape, shape],
            [(10, 112, 384), (10, 64, 384)],
            smem=(4, 5),
        )
        dirn, sums = local_call(
            direction_kernel, exchange(corr) + (total, geo, stiff, wjk), [shape, (8, 128)], []
        )
        sums = device_sum(sums, False, step)
        u, res = local_call(
            next_kernel, (u, dirn, sums) + consts, [shape, shape], [(12, 64, 384)]
        )
    corner = jnp.dot(
        jnp.asarray(CORNER, F32), res.reshape(512, 384), precision=lax.Precision.HIGHEST
    )
    corner = corner.reshape(8, 3, 128).transpose(0, 2, 1).reshape(1024, 3)
    owners = wide_count * narrow_count
    share = AROUND_DEV * (RADIAL + 1)
    ids = corner_vertex[:, inverse_slot].reshape(-1)
    full = jax.ops.segment_sum(corner, ids, num_segments=owners * share).T
    blocks = full.reshape(3, wide_count, narrow_count, share).transpose(2, 1, 0, 3)
    blocks = jnp.pad(blocks, ((0, 0), (0, 0), (0, 5), (0, 256 - share)))
    coarse = device_sum(blocks, True, STEPS)[0:3, 0:share]
    out = u.reshape(512, 3, 128).transpose(1, 0, 2)[:, :, slot_of]
    return out, coarse


def solution(mesh):
    return jax.shard_map(
        shards,
        mesh=mesh,
        in_specs=(
            P(None, None, ("wide", "narrow")),
            P(("wide", "narrow"), None),
            P(None, ("wide", "narrow")),
            P("wide"),
            P(),
            P(),
            P(),
            P(),
        ),
        out_specs=(P(None, None, ("wide", "narrow")), P(None, ("wide", "narrow"))),
        check_vma=False,
    )
```

```python
from functools import partial

import jax
import jax.numpy as jnp
import ml_dtypes
import numpy as np
from jax import lax
from jax.experimental import pallas as pl
from jax.experimental.pallas import tpu as pltpu
from jax.sharding import PartitionSpec as P

AROUND_DEV = 8
RADIAL = 16
STEPS = 2
SIGMA = 4.0
VISCOSITY = 0.05
LIMIT = 48 * 1024 * 1024
MESH = pl.DeviceIdType.MESH
F32 = jnp.float32
BF16 = jnp.bfloat16


def node_tables():
    gll_nodes = np.array(
        [
            -1.0,
            -0.8717401485096066,
            -0.5917001814331423,
            -0.2092992179024789,
            0.2092992179024789,
            0.5917001814331423,
            0.8717401485096066,
            1.0,
        ]
    )
    gll_weights = np.array(
        [
            1.0 / 28.0,
            0.2107042271435061,
            0.3411226924835044,
            0.4124587946587038,
            0.4124587946587038,
            0.3411226924835044,
            0.2107042271435061,
            1.0 / 28.0,
        ]
    )
    bary_scale = np.array(
        [
            np.prod(
                [
                    gll_nodes[target] - gll_nodes[partner]
                    for partner in range(8)
                    if partner != target
                ]
            )
            for target in range(8)
        ]
    )
    derivative = np.zeros((8, 8))
    for target in range(8):
        for source in range(8):
            if target != source:
                derivative[target, source] = bary_scale[target] / (
                    bary_scale[source] * (gll_nodes[target] - gll_nodes[source])
                )
        derivative[target, target] = -np.sum(derivative[target])
    fine_nodes = np.array(
        [
            -0.9815606342467192,
            -0.9041172563704749,
            -0.7699026741943047,
            -0.5873179542866175,
            -0.3678314989981802,
            -0.1252334085114689,
            0.1252334085114689,
            0.3678314989981802,
            0.5873179542866175,
            0.7699026741943047,
            0.9041172563704749,
            0.9815606342467192,
        ]
    )
    fine_weights = np.array(
        [
            0.0471753363865118,
            0.1069393259953184,
            0.1600783285433462,
            0.2031674267230659,
            0.2334925365383548,
            0.2491470458134028,
            0.2491470458134028,
            0.2334925365383548,
            0.2031674267230659,
            0.1600783285433462,
            0.1069393259953184,
            0.0471753363865118,
        ]
    )
    interp = np.ones((12, 8))
    for source in range(8):
        for partner in range(8):
            if partner != source:
                interp[:, source] = (
                    interp[:, source]
                    * (fine_nodes - gll_nodes[partner])
                    / (gll_nodes[source] - gll_nodes[partner])
                )
    linear = np.stack([(1.0 - gll_nodes) / 2.0, (1.0 + gll_nodes) / 2.0])
    return derivative, interp, linear, gll_weights, fine_weights


def stack_const(matrix):
    high = matrix.astype(ml_dtypes.bfloat16)
    low = (matrix - high.astype(np.float64)).astype(ml_dtypes.bfloat16)
    return np.concatenate([high, low, high], axis=1)


DERIV, INTERP, LINEAR, WGLL, WFINE = node_tables()
INTERP_DERIV = INTERP @ DERIV
BEND = DERIV.T @ np.diag(WGLL) @ DERIV
FORWARD = stack_const(
    np.concatenate(
        [np.kron(INTERP, INTERP), np.kron(INTERP_DERIV, INTERP), np.kron(INTERP, INTERP_DERIV)]
    )
)
BACKWARD = stack_const((np.kron(INTERP, INTERP) * np.kron(WFINE, WFINE)[:, None]).T)
LINEAR_JK = stack_const(np.concatenate([np.kron(LINEAR[b], LINEAR[c])[None] for b in range(2) for c in range(2)] + [np.zeros((4, 64))]))
STIFF = stack_const(
    np.concatenate([np.kron(BEND, np.diag(WGLL)), np.kron(np.diag(WGLL), BEND)])
)
WEIGHT_JK = np.kron(WGLL, WGLL).astype(np.float32)


def split_rows(x):
    high = x.astype(BF16)
    low = (x - high.astype(F32)).astype(BF16)
    return jnp.concatenate([high, high, low], axis=0)


def split_cols(x):
    high = x.astype(BF16)
    low = (x - high.astype(F32)).astype(BF16)
    return jnp.concatenate([high, low, high], axis=1)


def mm(a, b):
    return jnp.dot(a, b, preferred_element_type=F32)


def combine(coefs, planes):
    total = None
    for coef, plane in zip(coefs, planes):
        term = plane * coef
        total = term if total is None else total + term
    return total


def lane_roll(x, shift):
    parts = [
        pltpu.roll(x[:, b : b + 128], shift, 1) for b in range(0, x.shape[1], 128)
    ]
    return jnp.concatenate(parts, axis=1)


def row_k(shape):
    return lax.broadcasted_iota(jnp.int32, shape, 0) % 8


def keep_mask(shape, low_in, high_in):
    k = row_k(shape)
    return jnp.where(k == 0, low_in, 1.0) * jnp.where(k == 7, high_in, 1.0)


def inverse_mult(shape, low_in, high_in, plane):
    k = row_k(shape)
    j = lax.broadcasted_iota(jnp.int32, shape, 0) // 8
    scale = jnp.where((j == 0) | (j == 7), 0.5, 1.0)
    scale = scale * jnp.where(k == 0, 1.0 - 0.5 * low_in, 1.0)
    scale = scale * jnp.where(k == 7, 1.0 - 0.5 * high_in, 1.0)
    return scale * 0.5 if plane in (0, 7) else scale


def around(mine, other, up):
    lane = lax.broadcasted_iota(jnp.int32, mine.shape, 1) % 128
    if up:
        return lane_roll(jnp.where(lane >= 128 - RADIAL, other, mine), RADIAL)
    return lane_roll(jnp.where(lane < RADIAL, other, mine), 128 - RADIAL)


def radial_sum(x, low_in, high_in):
    rows = x.shape[0]
    k = row_k(x.shape)
    below = lane_roll(pltpu.roll(x, rows - 7, 0), 1)
    above = lane_roll(pltpu.roll(x, 7, 0), 127)
    return x + jnp.where(k == 0, below * low_in, 0.0) + jnp.where(k == 7, above * high_in, 0.0)


def pack_faces(y, blocks, start):
    lane = lax.broadcasted_iota(jnp.int32, (8, 128), 1) // RADIAL
    packed = jnp.zeros((8, 128), F32)
    for q, (row, c) in enumerate(blocks):
        piece = y[row : row + 8, 128 * c : 128 * c + 128]
        packed = jnp.where(lane == q, pltpu.roll(piece, (RADIAL * q - start) % 128, 1), packed)
    return packed


def unpack_faces(packed, first, channels, start):
    return jnp.concatenate(
        [
            pltpu.roll(packed, (start - RADIAL * (first + c)) % 128, 1) if start != RADIAL * (first + c) else packed
            for c in range(channels)
        ],
        axis=1,
    )


def join_kernel(wide, x_ref, below_ref, above_ref, y_ref, prev_ref, next_ref):
    channels = x_ref.shape[2] // 128
    planes = [x_ref[i] for i in range(8)]
    if wide:
        planes = [below_ref[0], planes[0] + below_ref[1]] + planes[1:7]
        planes = planes + [x_ref[7] + above_ref[0], above_ref[1]]
        low_rows, high_rows = (0, 8), (48, 56)
    else:
        planes = [planes[0] + below_ref[0]] + planes[1:7] + [planes[7] + above_ref[0]]
        low_rows, high_rows = (0,), (56,)
    low = [(row, c) for row in low_rows for c in range(channels)]
    high = [(row, c) for row in high_rows for c in range(channels)]
    for i, plane in enumerate(planes):
        y_ref[i] = plane
        prev_ref[i] = pack_faces(plane, low, 0)
        next_ref[i] = pack_faces(plane, high, 128 - RADIAL)


def exact_parts(x):
    high = x.astype(BF16)
    rest = x - high.astype(F32)
    middle = rest.astype(BF16)
    return high, middle, (rest - middle.astype(F32)).astype(BF16)


def enter_kernel(vel_ref, slot_ref, mass_ref, field_ref):
    rows = lax.broadcasted_iota(jnp.int32, (128, 128), 0)
    place = jnp.where(rows == slot_ref[...], 1.0, 0.0).astype(BF16)
    for c in range(3):
        parts = exact_parts(vel_ref[c])
        moved = [
            lax.dot_general(p, place, (((1,), (1,)), ((), ())), preferred_element_type=F32)
            for p in parts
        ]
        lanes = slice(128 * c, 128 * c + 128)
        field_ref[:, lanes] = ((moved[0] + moved[1]) + moved[2]) * mass_ref[...]
    field_ref[:, 384:512] = mass_ref[...]


def leave_kernel(owners, u_ref, res_ref, slot_ref, ids_ref, ljk_ref, out_ref, full_ref):
    rows = lax.broadcasted_iota(jnp.int32, (128, 128), 0)
    place = jnp.where(rows == slot_ref[...], 1.0, 0.0).astype(BF16)
    for c in range(3):
        lanes = slice(128 * c, 128 * c + 128)
        moved = [mm(p, place) for p in exact_parts(u_ref[:, lanes])]
        out_ref[c] = (moved[0] + moved[1]) + moved[2]
    planes = [res_ref[64 * i : 64 * i + 64] for i in range(8)]
    corners = []
    for a in range(2):
        flat = combine([float(v) for v in LINEAR[a]], planes)
        corners.append(mm(ljk_ref[...], split_rows(flat))[0:4])
    corners = jnp.concatenate(corners, axis=0)
    share = AROUND_DEV * (RADIAL + 1)
    ids = ids_ref[...]
    owner = ids // share
    spot = ids - owner * share
    owner_rows = lax.broadcasted_iota(jnp.int32, (owners, 128), 0)
    spot_rows = lax.broadcasted_iota(jnp.int32, (256, 128), 0)
    left, right = [], []
    for q in range(8):
        hit = owner_rows == owner[q : q + 1]
        terms = []
        for c in range(3):
            value = corners[q : q + 1, 128 * c : 128 * c + 128]
            terms.append(jnp.where(hit, value, 0.0))
        left.append(jnp.concatenate(terms, axis=0))
        right.append(jnp.where(spot_rows == spot[q : q + 1], 1.0, 0.0).astype(BF16))
    left = jnp.concatenate(left, axis=1)
    right = jnp.concatenate(right, axis=1)
    parts = [
        lax.dot_general(p, right, (((1,), (1,)), ((), ())), preferred_element_type=F32)
        for p in exact_parts(left)
    ]
    full_ref[...] = (parts[0] + parts[1]) + parts[2]


def around_sum(y, prev_high, next_low):
    low = y[0:8] + around(y[56:64], prev_high, True)
    high = y[56:64] + around(y[0:8], next_low, False)
    return low, high


def stiffness(planes, index, geo, stiff, weight_jk):
    mixed = mm(stiff, split_rows(planes[index]))
    along = combine([float(v) for v in BEND[index]], planes) * weight_jk
    inv0, inv1, inv2 = geo[0:1], geo[1:2], geo[2:3]
    across = mixed[0:64] * (inv1 * inv1) + mixed[64:128] * (inv2 * inv2)
    return along * (inv0 * inv0) + across * float(WGLL[index])


def write_residual(u, geo, fwd_ref, back_ref, stiff_ref, wjk, out_ref, fine_ref):
    inv = [geo[d : d + 1, 0:128] for d in range(3)]
    volume, low_in, high_in = geo[3:4], geo[4:5], geo[5:6]
    fwd = fwd_ref[...]
    back = back_ref[...]
    stiff = stiff_ref[...]
    planes = [u[i] for i in range(8)]
    for a in range(12):
        plain = combine([float(v) for v in INTERP[a]], planes)
        slope = combine([float(v) for v in INTERP_DERIV[a]], planes)
        fine = mm(fwd, split_rows(plain))
        along = mm(fwd[0:144], split_rows(slope))
        speed = [fine[0:144, 128 * d : 128 * d + 128] * inv[d] for d in range(3)]
        terms = []
        for c in range(3):
            lanes = slice(128 * c, 128 * c + 128)
            terms.append(
                speed[0] * along[:, lanes]
                + speed[1] * fine[144:288, lanes]
                + speed[2] * fine[288:432, lanes]
            )
        fine_ref[a] = mm(back, split_rows(jnp.concatenate(terms, axis=1)))
    keep = keep_mask((64, 384), low_in, high_in)
    for i in range(8):
        advect = combine(
            [float(v) for v in INTERP[:, i] * WFINE], [fine_ref[a] for a in range(12)]
        )
        bend = stiffness(planes, i, geo, stiff, wjk)
        out_ref[i] = -(advect + VISCOSITY * bend) * volume * keep


def first_kernel(y_ref, prev_ref, next_ref, geo_ref, fwd, back, stiff, wjk_ref, u_ref, res_ref, fine_ref):
    geo = geo_ref[...]
    low4 = jnp.concatenate([geo[4:5], geo[4:5, 0:128]], axis=1)
    high4 = jnp.concatenate([geo[5:6], geo[5:6, 0:128]], axis=1)
    keep = keep_mask((64, 384), geo[4:5], geo[5:6])
    for i in range(8):
        y = y_ref[i]
        low, high = around_sum(y, unpack_faces(prev_ref[i], 0, 4, 112), unpack_faces(next_ref[i], 0, 4, 0))
        total = radial_sum(jnp.concatenate([low, y[8:56], high], axis=0), low4, high4)
        mass = total[:, 384:512]
        u_ref[i] = total[:, 0:384] / jnp.concatenate([mass, mass, mass], axis=1) * keep
    write_residual(u_ref, geo, fwd, back, stiff, wjk_ref[...], res_ref, fine_ref)


def next_kernel(u_in, dirn_ref, sums_ref, geo_ref, fwd, back, stiff, wjk_ref, u_ref, res_ref, fine_ref):
    sums = sums_ref[...]
    step = jnp.sum(sums[0:1], axis=1, keepdims=True) / jnp.sum(sums[1:2], axis=1, keepdims=True)
    for i in range(8):
        u_ref[i] = u_in[i] + dirn_ref[i] * step
    write_residual(u_ref, geo_ref[...], fwd, back, stiff, wjk_ref[...], res_ref, fine_ref)


def solve_kernel(y_ref, prev_ref, next_ref, geo_ref, s_ref, lam_ref, into_ref, back_ref, lam2_ref, res_ref, corr_ref, ext_ref, spec_ref):
    geo = geo_ref[...]
    volume, low_in, high_in = geo[3:4], geo[4:5], geo[5:6]
    into = split_cols(into_ref[...])
    back = split_cols(back_ref[...])
    for i in range(10):
        y = y_ref[i]
        prev, following = prev_ref[i], next_ref[i]
        low, high = around_sum(y, unpack_faces(prev, 3, 3, 112), unpack_faces(following, 0, 3, 0))
        outer_low = around(y[48:56], unpack_faces(prev, 0, 3, 112), True)
        outer_high = around(y[8:16], unpack_faces(following, 3, 3, 0), False)
        wide = jnp.concatenate([outer_low, low, y[8:56], high, outer_high], axis=0)
        wide = radial_sum(wide, low_in, high_in)
        if 1 <= i <= 8:
            res_ref[i - 1] = wide[8:72]
        k = row_k(wide.shape)
        halo = jnp.where(k == 6, lane_roll(wide, 1) * low_in, 0.0)
        halo = jnp.where(k == 1, lane_roll(wide, 127) * high_in, halo)
        ext_ref[i] = mm(into, split_rows(jnp.concatenate([wide, halo], axis=0)))
    sq = [geo[d : d + 1] * geo[d : d + 1] for d in range(3)]
    lam2 = lam2_ref[...]
    cross = (lam2[:, 0:1] * sq[1] + lam2[:, 1:2] * sq[2]) * VISCOSITY + SIGMA
    for a in range(10):
        spectral = combine([s_ref[i, a] for i in range(10)], [ext_ref[i] for i in range(10)])
        scaling = volume * (cross + (VISCOSITY * lam_ref[a]) * sq[0])
        spec_ref[a] = mm(back, split_rows(spectral / scaling))
    for i in range(8):
        corr = combine([s_ref[i + 1, a] for a in range(10)], [spec_ref[a] for a in range(10)])
        corr_ref[i] = corr * inverse_mult((64, 384), low_in, high_in, i)


def direction_kernel(y_ref, prev_ref, next_ref, res_ref, geo_ref, stiff_ref, wjk_ref, dirn_ref, sums_ref):
    geo = geo_ref[...]
    volume, low_in, high_in = geo[3:4], geo[4:5], geo[5:6]
    wjk = wjk_ref[...]
    stiff = stiff_ref[...]
    keep = keep_mask((64, 384), low_in, high_in)
    numer = jnp.zeros((64, 384), F32)
    for i in range(8):
        y = y_ref[i]
        low, high = around_sum(y, unpack_faces(prev_ref[i], 0, 3, 112), unpack_faces(next_ref[i], 0, 3, 0))
        total = radial_sum(jnp.concatenate([low, y[8:56], high], axis=0), low_in, high_in)
        total = total * keep
        dirn_ref[i] = total
        numer = numer + res_ref[i] * total * inverse_mult((64, 384), low_in, high_in, i)
    planes = [dirn_ref[i] for i in range(8)]
    denom = jnp.zeros((64, 384), F32)
    for i in range(8):
        bend = stiffness(planes, i, geo, stiff, wjk)
        mass = wjk * float(SIGMA * WGLL[i])
        denom = denom + planes[i] * (mass * planes[i] + VISCOSITY * bend)
    denom = denom * volume

    def fold(x):
        x = jnp.sum(x, axis=0, keepdims=True)
        return x[:, 0:128] + x[:, 128:256] + x[:, 256:384]

    row = lax.broadcasted_iota(jnp.int32, (8, 128), 0)
    sums_ref[...] = jnp.where(row == 0, fold(numer), jnp.where(row == 1, fold(denom), 0.0))


def sum_kernel(wide, narrow, scatter, x_ref, o_ref, from_narrow, part, from_wide, s1, r1, s2, r2):
    w, n = lax.axis_index("wide"), lax.axis_index("narrow")
    barrier = pltpu.get_barrier_semaphore()
    for k in range(1, narrow):
        pl.semaphore_signal(barrier, inc=1, device_id=(w, (n + k) % narrow), device_id_type=MESH)
    for k in range(1, wide):
        pl.semaphore_signal(barrier, inc=1, device_id=((w + k) % wide, n), device_id_type=MESH)
    pl.semaphore_wait(barrier, narrow + wide - 2)
    copies = []
    for k in range(1, narrow):
        peer = (n + k) % narrow
        copy = pltpu.make_async_remote_copy(
            src_ref=x_ref.at[peer] if scatter else x_ref,
            dst_ref=from_narrow.at[k - 1],
            send_sem=s1.at[k - 1],
            recv_sem=r1.at[k - 1],
            device_id=(w, peer),
            device_id_type=MESH,
        )
        copy.start()
        copies.append(copy)
    total = x_ref[n] if scatter else x_ref[...]
    for k, copy in enumerate(copies):
        copy.wait()
        total = total + from_narrow[k]
    part[...] = total
    copies = []
    for k in range(1, wide):
        peer = (w + k) % wide
        copy = pltpu.make_async_remote_copy(
            src_ref=part.at[peer] if scatter else part,
            dst_ref=from_wide.at[k - 1],
            send_sem=s2.at[k - 1],
            recv_sem=r2.at[k - 1],
            device_id=(peer, n),
            device_id_type=MESH,
        )
        copy.start()
        copies.append(copy)
    total = part[w] if scatter else part[...]
    for k, copy in enumerate(copies):
        copy.wait()
        total = total + from_wide[k]
    o_ref[...] = total


def device_sum(x, scatter, ident):
    wide, narrow = lax.axis_size("wide"), lax.axis_size("narrow")
    middle = x.shape[1:] if scatter else x.shape
    last = middle[1:] if scatter else x.shape
    return pl.pallas_call(
        partial(sum_kernel, wide, narrow, scatter),
        out_shape=jax.ShapeDtypeStruct(last, F32),
        in_specs=[pl.BlockSpec(memory_space=pltpu.VMEM)],
        out_specs=pl.BlockSpec(memory_space=pltpu.VMEM),
        scratch_shapes=[
            pltpu.VMEM((narrow - 1,) + middle, F32),
            pltpu.VMEM(middle, F32),
            pltpu.VMEM((wide - 1,) + last, F32),
            pltpu.SemaphoreType.DMA((narrow - 1,)),
            pltpu.SemaphoreType.DMA((narrow - 1,)),
            pltpu.SemaphoreType.DMA((wide - 1,)),
            pltpu.SemaphoreType.DMA((wide - 1,)),
        ],
        compiler_params=pltpu.CompilerParams(
            collective_id=ident, has_side_effects=True, vmem_limit_bytes=LIMIT
        ),
    )(x)


def local_call(body, args, outs, scratch, smem=()):
    return pl.pallas_call(
        body,
        out_shape=[jax.ShapeDtypeStruct(s, F32) for s in outs],
        in_specs=[
            pl.BlockSpec(memory_space=pltpu.SMEM if p in smem else pltpu.VMEM)
            for p in range(len(args))
        ],
        out_specs=[pl.BlockSpec(memory_space=pltpu.VMEM)] * len(outs),
        scratch_shapes=[pltpu.VMEM(s, F32) for s in scratch],
        compiler_params=pltpu.CompilerParams(vmem_limit_bytes=LIMIT),
    )(*args)


def swap(axis, to_prev, to_next):
    count = lax.axis_size(axis)
    from_prev = lax.ppermute(to_next, axis, [(i, (i + 1) % count) for i in range(count)])
    from_next = lax.ppermute(to_prev, axis, [((i + 1) % count, i) for i in range(count)])
    return from_prev, from_next


def exchange(x, wide=False):
    width = 2 if wide else 1
    below, above = swap("wide", x[0:width], x[8 - width : 8])
    depth = 10 if wide else 8
    y, low, high = local_call(
        partial(join_kernel, wide),
        (x, below, above),
        [(depth, 64, x.shape[2]), (depth, 8, 128), (depth, 8, 128)],
        [],
    )
    return (y,) + swap("narrow", low, high)


def shards(
    velocity,
    element_slot,
    corner_vertex,
    axial_size,
    arc_size,
    radial_size,
    fdm_vectors,
    fdm_values,
):
    wide_count, narrow_count = lax.axis_size("wide"), lax.axis_size("narrow")
    slot_of = element_slot[0]
    inverse_slot = jnp.zeros((128,), jnp.int32).at[slot_of].set(jnp.arange(128, dtype=jnp.int32))
    ids = corner_vertex[:, inverse_slot]
    er = jnp.arange(128) % RADIAL
    hz = jnp.broadcast_to(axial_size, (128,))
    ht = jnp.tile(arc_size, AROUND_DEV)
    hr = jnp.tile(radial_size, AROUND_DEV)
    volume = hz * ht * hr / 8.0
    zero = jnp.zeros((128,), F32)
    rows = [2.0 / hz, 2.0 / ht, 2.0 / hr, volume]
    rows += [jnp.where(er > 0, 1.0, 0.0), jnp.where(er < RADIAL - 1, 1.0, 0.0), zero, zero]
    geo = jnp.tile(jnp.stack(rows).astype(F32), (1, 3))
    fwd, back, stiff = jnp.asarray(FORWARD), jnp.asarray(BACKWARD), jnp.asarray(STIFF)
    wjk = jnp.broadcast_to(jnp.asarray(WEIGHT_JK)[:, None], (64, 384))
    consts = (geo, fwd, back, stiff, wjk)

    transform = fdm_vectors.T.reshape(10, 1, 10, 1) * fdm_vectors.T.reshape(1, 10, 1, 10)
    own = transform[..., 1:9].reshape(100, 80)
    halo = jnp.zeros((10, 10, 10, 8), F32)
    halo = halo.at[..., 6].set(transform[..., 0]).at[..., 1].set(transform[..., 9])
    into = jnp.pad(jnp.concatenate([own, halo.reshape(100, 80)], axis=1), ((0, 12), (0, 0)))
    inner = fdm_vectors[1:9]
    outof = (inner.reshape(8, 1, 10, 1) * inner.reshape(1, 8, 1, 10)).reshape(64, 100)
    outof = jnp.pad(outof, ((0, 0), (0, 12)))
    lam2 = jnp.stack([jnp.repeat(fdm_values, 10), jnp.tile(fdm_values, 10)], axis=1)
    lam2 = jnp.pad(lam2, ((0, 12), (0, 126)), constant_values=1.0)

    mass = (np.kron(WGLL, np.kron(WGLL, WGLL)).astype(np.float32))[:, None] * volume[None]
    (field,) = local_call(enter_kernel, (velocity, element_slot, mass), [(512, 512)], [])
    field = field.reshape(8, 64, 512)

    shape = (8, 64, 384)
    u, res = local_call(first_kernel, exchange(field) + consts, [shape, shape], [(12, 64, 384)])
    for step in range(STEPS):
        total, corr = local_call(
            solve_kernel,
            exchange(res, True) + (geo, fdm_vectors, fdm_values, into, outof, lam2),
            [shape, shape],
            [(10, 112, 384), (10, 64, 384)],
            smem=(4, 5),
        )
        dirn, sums = local_call(
            direction_kernel, exchange(corr) + (total, geo, stiff, wjk), [shape, (8, 128)], []
        )
        sums = device_sum(sums, False, step)
        u, res = local_call(
            next_kernel, (u, dirn, sums) + consts, [shape, shape], [(12, 64, 384)]
        )
    owners = wide_count * narrow_count
    share = AROUND_DEV * (RADIAL + 1)
    out, full = local_call(
        partial(leave_kernel, owners),
        (u.reshape(512, 384), res.reshape(512, 384), element_slot, ids, jnp.asarray(LINEAR_JK)),
        [(3, 512, 128), (3 * owners, 256)],
        [],
    )
    blocks = full.reshape(3, wide_count, narrow_count, 256).transpose(2, 1, 0, 3)
    blocks = jnp.pad(blocks, ((0, 0), (0, 0), (0, 5), (0, 0)))
    coarse = device_sum(blocks, True, STEPS)[0:3, 0:share]
    return out, coarse


def solution(mesh):
    return jax.shard_map(
        shards,
        mesh=mesh,
        in_specs=(
            P(None, None, ("wide", "narrow")),
            P(("wide", "narrow"), None),
            P(None, ("wide", "narrow")),
            P("wide"),
            P(),
            P(),
            P(),
            P(),
        ),
        out_specs=(P(None, None, ("wide", "narrow")), P(None, ("wide", "narrow"))),
        check_vma=False,
    )
```

```python
from functools import partial

import jax
import jax.numpy as jnp
import ml_dtypes
import numpy as np
from jax import lax
from jax.experimental import pallas as pl
from jax.experimental.pallas import tpu as pltpu
from jax.sharding import PartitionSpec as P

AROUND_DEV = 8
RADIAL = 16
STEPS = 2
SIGMA = 4.0
VISCOSITY = 0.05
LIMIT = 48 * 1024 * 1024
MESH = pl.DeviceIdType.MESH
F32 = jnp.float32
BF16 = jnp.bfloat16


def node_tables():
    gll_nodes = np.array(
        [
            -1.0,
            -0.8717401485096066,
            -0.5917001814331423,
            -0.2092992179024789,
            0.2092992179024789,
            0.5917001814331423,
            0.8717401485096066,
            1.0,
        ]
    )
    gll_weights = np.array(
        [
            1.0 / 28.0,
            0.2107042271435061,
            0.3411226924835044,
            0.4124587946587038,
            0.4124587946587038,
            0.3411226924835044,
            0.2107042271435061,
            1.0 / 28.0,
        ]
    )
    bary_scale = np.array(
        [
            np.prod(
                [
                    gll_nodes[target] - gll_nodes[partner]
                    for partner in range(8)
                    if partner != target
                ]
            )
            for target in range(8)
        ]
    )
    derivative = np.zeros((8, 8))
    for target in range(8):
        for source in range(8):
            if target != source:
                derivative[target, source] = bary_scale[target] / (
                    bary_scale[source] * (gll_nodes[target] - gll_nodes[source])
                )
        derivative[target, target] = -np.sum(derivative[target])
    fine_nodes = np.array(
        [
            -0.9815606342467192,
            -0.9041172563704749,
            -0.7699026741943047,
            -0.5873179542866175,
            -0.3678314989981802,
            -0.1252334085114689,
            0.1252334085114689,
            0.3678314989981802,
            0.5873179542866175,
            0.7699026741943047,
            0.9041172563704749,
            0.9815606342467192,
        ]
    )
    fine_weights = np.array(
        [
            0.0471753363865118,
            0.1069393259953184,
            0.1600783285433462,
            0.2031674267230659,
            0.2334925365383548,
            0.2491470458134028,
            0.2491470458134028,
            0.2334925365383548,
            0.2031674267230659,
            0.1600783285433462,
            0.1069393259953184,
            0.0471753363865118,
        ]
    )
    interp = np.ones((12, 8))
    for source in range(8):
        for partner in range(8):
            if partner != source:
                interp[:, source] = (
                    interp[:, source]
                    * (fine_nodes - gll_nodes[partner])
                    / (gll_nodes[source] - gll_nodes[partner])
                )
    linear = np.stack([(1.0 - gll_nodes) / 2.0, (1.0 + gll_nodes) / 2.0])
    return derivative, interp, linear, gll_weights, fine_weights


def stack_const(matrix):
    high = matrix.astype(ml_dtypes.bfloat16)
    low = (matrix - high.astype(np.float64)).astype(ml_dtypes.bfloat16)
    return np.concatenate([high, low, high], axis=1)


DERIV, INTERP, LINEAR, WGLL, WFINE = node_tables()
INTERP_DERIV = INTERP @ DERIV
BEND = DERIV.T @ np.diag(WGLL) @ DERIV
FORWARD = stack_const(
    np.concatenate(
        [np.kron(INTERP, INTERP), np.kron(INTERP_DERIV, INTERP), np.kron(INTERP, INTERP_DERIV)]
    )
)
BACKWARD = stack_const((np.kron(INTERP, INTERP) * np.kron(WFINE, WFINE)[:, None]).T)
LINEAR_JK = stack_const(np.concatenate([np.kron(LINEAR[b], LINEAR[c])[None] for b in range(2) for c in range(2)] + [np.zeros((4, 64))]))
STIFF = stack_const(
    np.concatenate([np.kron(BEND, np.diag(WGLL)), np.kron(np.diag(WGLL), BEND)])
)
WEIGHT_JK = np.kron(WGLL, WGLL).astype(np.float32)


def split_rows(x):
    high = x.astype(BF16)
    low = (x - high.astype(F32)).astype(BF16)
    return jnp.concatenate([high, high, low], axis=0)


def split_cols(x):
    high = x.astype(BF16)
    low = (x - high.astype(F32)).astype(BF16)
    return jnp.concatenate([high, low, high], axis=1)


def mm(a, b):
    return jnp.dot(a, b, preferred_element_type=F32)


def combine(coefs, planes):
    total = None
    for coef, plane in zip(coefs, planes):
        term = plane * coef
        total = term if total is None else total + term
    return total


def lane_roll(x, shift):
    parts = [
        pltpu.roll(x[:, b : b + 128], shift, 1) for b in range(0, x.shape[1], 128)
    ]
    return jnp.concatenate(parts, axis=1)


def row_k(shape):
    return lax.broadcasted_iota(jnp.int32, shape, 0) % 8


def keep_mask(shape, low_in, high_in):
    k = row_k(shape)
    return jnp.where(k == 0, low_in, 1.0) * jnp.where(k == 7, high_in, 1.0)


def inverse_mult(shape, low_in, high_in, plane):
    k = row_k(shape)
    j = lax.broadcasted_iota(jnp.int32, shape, 0) // 8
    scale = jnp.where((j == 0) | (j == 7), 0.5, 1.0)
    scale = scale * jnp.where(k == 0, 1.0 - 0.5 * low_in, 1.0)
    scale = scale * jnp.where(k == 7, 1.0 - 0.5 * high_in, 1.0)
    return scale * 0.5 if plane in (0, 7) else scale


def around(mine, other, up):
    lane = lax.broadcasted_iota(jnp.int32, mine.shape, 1) % 128
    if up:
        return lane_roll(jnp.where(lane >= 128 - RADIAL, other, mine), RADIAL)
    return lane_roll(jnp.where(lane < RADIAL, other, mine), 128 - RADIAL)


def radial_sum(x, low_in, high_in):
    rows = x.shape[0]
    k = row_k(x.shape)
    below = lane_roll(pltpu.roll(x, rows - 7, 0), 1)
    above = lane_roll(pltpu.roll(x, 7, 0), 127)
    return x + jnp.where(k == 0, below * low_in, 0.0) + jnp.where(k == 7, above * high_in, 0.0)


def pack_faces(y, blocks, start):
    lane = lax.broadcasted_iota(jnp.int32, (8, 128), 1) // RADIAL
    packed = jnp.zeros((8, 128), F32)
    for q, (row, c) in enumerate(blocks):
        piece = y[row : row + 8, 128 * c : 128 * c + 128]
        packed = jnp.where(lane == q, pltpu.roll(piece, (RADIAL * q - start) % 128, 1), packed)
    return packed


def unpack_faces(packed, first, channels, start):
    return jnp.concatenate(
        [
            pltpu.roll(packed, (start - RADIAL * (first + c)) % 128, 1) if start != RADIAL * (first + c) else packed
            for c in range(channels)
        ],
        axis=1,
    )


def join_kernel(wide, x_ref, below_ref, above_ref, y_ref, prev_ref, next_ref):
    channels = x_ref.shape[2] // 128
    planes = [x_ref[i] for i in range(8)]
    if wide:
        planes = [below_ref[0], planes[0] + below_ref[1]] + planes[1:7]
        planes = planes + [x_ref[7] + above_ref[0], above_ref[1]]
        low_rows, high_rows = (0, 8), (48, 56)
    else:
        planes = [planes[0] + below_ref[0]] + planes[1:7] + [planes[7] + above_ref[0]]
        low_rows, high_rows = (0,), (56,)
    low = [(row, c) for row in low_rows for c in range(channels)]
    high = [(row, c) for row in high_rows for c in range(channels)]
    for i, plane in enumerate(planes):
        y_ref[i] = plane
        prev_ref[i] = pack_faces(plane, low, 0)
        next_ref[i] = pack_faces(plane, high, 128 - RADIAL)


def exact_parts(x):
    high = x.astype(BF16)
    rest = x - high.astype(F32)
    middle = rest.astype(BF16)
    return high, middle, (rest - middle.astype(F32)).astype(BF16)


def enter_kernel(vel_ref, slot_ref, mass_ref, field_ref):
    rows = lax.broadcasted_iota(jnp.int32, (128, 128), 0)
    place = jnp.where(rows == slot_ref[...], 1.0, 0.0).astype(BF16)
    for c in range(3):
        parts = exact_parts(vel_ref[c])
        moved = [
            lax.dot_general(p, place, (((1,), (1,)), ((), ())), preferred_element_type=F32)
            for p in parts
        ]
        lanes = slice(128 * c, 128 * c + 128)
        field_ref[:, lanes] = ((moved[0] + moved[1]) + moved[2]) * mass_ref[...]
    field_ref[:, 384:512] = mass_ref[...]


def leave_kernel(owners, u_ref, res_ref, slot_ref, ids_ref, ljk_ref, out_ref, full_ref):
    rows = lax.broadcasted_iota(jnp.int32, (128, 128), 0)
    place = jnp.where(rows == slot_ref[...], 1.0, 0.0).astype(BF16)
    for c in range(3):
        lanes = slice(128 * c, 128 * c + 128)
        moved = [mm(p, place) for p in exact_parts(u_ref[:, lanes])]
        out_ref[c] = (moved[0] + moved[1]) + moved[2]
    planes = [res_ref[64 * i : 64 * i + 64] for i in range(8)]
    corners = []
    for a in range(2):
        flat = combine([float(v) for v in LINEAR[a]], planes)
        corners.append(mm(ljk_ref[...], split_rows(flat))[0:4])
    corners = jnp.concatenate(corners, axis=0)
    stored = []
    for c in range(3):
        moved = [mm(p, place) for p in exact_parts(corners[:, 128 * c : 128 * c + 128])]
        stored.append((moved[0] + moved[1]) + moved[2])
    corners = jnp.concatenate(stored, axis=1)
    share = AROUND_DEV * (RADIAL + 1)
    ids = ids_ref[...]
    owner = ids // share
    spot = ids - owner * share
    owner_rows = lax.broadcasted_iota(jnp.int32, (owners, 128), 0)
    spot_rows = lax.broadcasted_iota(jnp.int32, (256, 128), 0)
    left, right = [], []
    for q in range(8):
        hit = owner_rows == owner[q : q + 1]
        terms = []
        for c in range(3):
            value = corners[q : q + 1, 128 * c : 128 * c + 128]
            terms.append(jnp.where(hit, value, 0.0))
        left.append(jnp.concatenate(terms, axis=0))
        right.append(jnp.where(spot_rows == spot[q : q + 1], 1.0, 0.0).astype(BF16))
    left = jnp.concatenate(left, axis=1)
    right = jnp.concatenate(right, axis=1)
    parts = [
        lax.dot_general(p, right, (((1,), (1,)), ((), ())), preferred_element_type=F32)
        for p in exact_parts(left)
    ]
    full_ref[...] = (parts[0] + parts[1]) + parts[2]


def around_sum(y, prev_high, next_low):
    low = y[0:8] + around(y[56:64], prev_high, True)
    high = y[56:64] + around(y[0:8], next_low, False)
    return low, high


def stiffness(planes, index, geo, stiff, weight_jk):
    mixed = mm(stiff, split_rows(planes[index]))
    along = combine([float(v) for v in BEND[index]], planes) * weight_jk
    inv0, inv1, inv2 = geo[0:1], geo[1:2], geo[2:3]
    across = mixed[0:64] * (inv1 * inv1) + mixed[64:128] * (inv2 * inv2)
    return along * (inv0 * inv0) + across * float(WGLL[index])


def write_residual(u, geo, fwd_ref, back_ref, stiff_ref, wjk, out_ref, fine_ref):
    inv = [geo[d : d + 1, 0:128] for d in range(3)]
    volume, low_in, high_in = geo[3:4], geo[4:5], geo[5:6]
    fwd = fwd_ref[...]
    back = back_ref[...]
    stiff = stiff_ref[...]
    planes = [u[i] for i in range(8)]
    for a in range(12):
        plain = combine([float(v) for v in INTERP[a]], planes)
        slope = combine([float(v) for v in INTERP_DERIV[a]], planes)
        fine = mm(fwd, split_rows(plain))
        along = mm(fwd[0:144], split_rows(slope))
        speed = [fine[0:144, 128 * d : 128 * d + 128] * inv[d] for d in range(3)]
        terms = []
        for c in range(3):
            lanes = slice(128 * c, 128 * c + 128)
            terms.append(
                speed[0] * along[:, lanes]
                + speed[1] * fine[144:288, lanes]
                + speed[2] * fine[288:432, lanes]
            )
        fine_ref[a] = mm(back, split_rows(jnp.concatenate(terms, axis=1)))
    keep = keep_mask((64, 384), low_in, high_in)
    for i in range(8):
        advect = combine(
            [float(v) for v in INTERP[:, i] * WFINE], [fine_ref[a] for a in range(12)]
        )
        bend = stiffness(planes, i, geo, stiff, wjk)
        out_ref[i] = -(advect + VISCOSITY * bend) * volume * keep


def first_kernel(y_ref, prev_ref, next_ref, geo_ref, fwd, back, stiff, wjk_ref, u_ref, res_ref, fine_ref):
    geo = geo_ref[...]
    low4 = jnp.concatenate([geo[4:5], geo[4:5, 0:128]], axis=1)
    high4 = jnp.concatenate([geo[5:6], geo[5:6, 0:128]], axis=1)
    keep = keep_mask((64, 384), geo[4:5], geo[5:6])
    for i in range(8):
        y = y_ref[i]
        low, high = around_sum(y, unpack_faces(prev_ref[i], 0, 4, 112), unpack_faces(next_ref[i], 0, 4, 0))
        total = radial_sum(jnp.concatenate([low, y[8:56], high], axis=0), low4, high4)
        mass = total[:, 384:512]
        u_ref[i] = total[:, 0:384] / jnp.concatenate([mass, mass, mass], axis=1) * keep
    write_residual(u_ref, geo, fwd, back, stiff, wjk_ref[...], res_ref, fine_ref)


def next_kernel(u_in, dirn_ref, sums_ref, geo_ref, fwd, back, stiff, wjk_ref, u_ref, res_ref, fine_ref):
    sums = sums_ref[...]
    step = jnp.sum(sums[0:1], axis=1, keepdims=True) / jnp.sum(sums[1:2], axis=1, keepdims=True)
    for i in range(8):
        u_ref[i] = u_in[i] + dirn_ref[i] * step
    write_residual(u_ref, geo_ref[...], fwd, back, stiff, wjk_ref[...], res_ref, fine_ref)


def solve_kernel(y_ref, prev_ref, next_ref, geo_ref, s_ref, lam_ref, into_ref, back_ref, lam2_ref, res_ref, corr_ref, ext_ref, spec_ref):
    geo = geo_ref[...]
    volume, low_in, high_in = geo[3:4], geo[4:5], geo[5:6]
    into = split_cols(into_ref[...])
    back = split_cols(back_ref[...])
    for i in range(10):
        y = y_ref[i]
        prev, following = prev_ref[i], next_ref[i]
        low, high = around_sum(y, unpack_faces(prev, 3, 3, 112), unpack_faces(following, 0, 3, 0))
        outer_low = around(y[48:56], unpack_faces(prev, 0, 3, 112), True)
        outer_high = around(y[8:16], unpack_faces(following, 3, 3, 0), False)
        wide = jnp.concatenate([outer_low, low, y[8:56], high, outer_high], axis=0)
        wide = radial_sum(wide, low_in, high_in)
        if 1 <= i <= 8:
            res_ref[i - 1] = wide[8:72]
        k = row_k(wide.shape)
        halo = jnp.where(k == 6, lane_roll(wide, 1) * low_in, 0.0)
        halo = jnp.where(k == 1, lane_roll(wide, 127) * high_in, halo)
        ext_ref[i] = mm(into, split_rows(jnp.concatenate([wide, halo], axis=0)))
    sq = [geo[d : d + 1] * geo[d : d + 1] for d in range(3)]
    lam2 = lam2_ref[...]
    cross = (lam2[:, 0:1] * sq[1] + lam2[:, 1:2] * sq[2]) * VISCOSITY + SIGMA
    for a in range(10):
        spectral = combine([s_ref[i, a] for i in range(10)], [ext_ref[i] for i in range(10)])
        scaling = volume * (cross + (VISCOSITY * lam_ref[a]) * sq[0])
        spec_ref[a] = mm(back, split_rows(spectral / scaling))
    for i in range(8):
        corr = combine([s_ref[i + 1, a] for a in range(10)], [spec_ref[a] for a in range(10)])
        corr_ref[i] = corr * inverse_mult((64, 384), low_in, high_in, i)


def direction_kernel(y_ref, prev_ref, next_ref, res_ref, geo_ref, stiff_ref, wjk_ref, dirn_ref, sums_ref):
    geo = geo_ref[...]
    volume, low_in, high_in = geo[3:4], geo[4:5], geo[5:6]
    wjk = wjk_ref[...]
    stiff = stiff_ref[...]
    keep = keep_mask((64, 384), low_in, high_in)
    numer = jnp.zeros((64, 384), F32)
    for i in range(8):
        y = y_ref[i]
        low, high = around_sum(y, unpack_faces(prev_ref[i], 0, 3, 112), unpack_faces(next_ref[i], 0, 3, 0))
        total = radial_sum(jnp.concatenate([low, y[8:56], high], axis=0), low_in, high_in)
        total = total * keep
        dirn_ref[i] = total
        numer = numer + res_ref[i] * total * inverse_mult((64, 384), low_in, high_in, i)
    planes = [dirn_ref[i] for i in range(8)]
    denom = jnp.zeros((64, 384), F32)
    for i in range(8):
        bend = stiffness(planes, i, geo, stiff, wjk)
        mass = wjk * float(SIGMA * WGLL[i])
        denom = denom + planes[i] * (mass * planes[i] + VISCOSITY * bend)
    denom = denom * volume

    def fold(x):
        x = jnp.sum(x, axis=0, keepdims=True)
        return x[:, 0:128] + x[:, 128:256] + x[:, 256:384]

    row = lax.broadcasted_iota(jnp.int32, (8, 128), 0)
    sums_ref[...] = jnp.where(row == 0, fold(numer), jnp.where(row == 1, fold(denom), 0.0))


def sum_kernel(wide, narrow, scatter, x_ref, o_ref, from_narrow, part, from_wide, s1, r1, s2, r2):
    w, n = lax.axis_index("wide"), lax.axis_index("narrow")
    barrier = pltpu.get_barrier_semaphore()
    for k in range(1, narrow):
        pl.semaphore_signal(barrier, inc=1, device_id=(w, (n + k) % narrow), device_id_type=MESH)
    for k in range(1, wide):
        pl.semaphore_signal(barrier, inc=1, device_id=((w + k) % wide, n), device_id_type=MESH)
    pl.semaphore_wait(barrier, narrow + wide - 2)
    copies = []
    for k in range(1, narrow):
        peer = (n + k) % narrow
        copy = pltpu.make_async_remote_copy(
            src_ref=x_ref.at[peer] if scatter else x_ref,
            dst_ref=from_narrow.at[k - 1],
            send_sem=s1.at[k - 1],
            recv_sem=r1.at[k - 1],
            device_id=(w, peer),
            device_id_type=MESH,
        )
        copy.start()
        copies.append(copy)
    total = x_ref[n] if scatter else x_ref[...]
    for k, copy in enumerate(copies):
        copy.wait()
        total = total + from_narrow[k]
    part[...] = total
    copies = []
    for k in range(1, wide):
        peer = (w + k) % wide
        copy = pltpu.make_async_remote_copy(
            src_ref=part.at[peer] if scatter else part,
            dst_ref=from_wide.at[k - 1],
            send_sem=s2.at[k - 1],
            recv_sem=r2.at[k - 1],
            device_id=(peer, n),
            device_id_type=MESH,
        )
        copy.start()
        copies.append(copy)
    total = part[w] if scatter else part[...]
    for k, copy in enumerate(copies):
        copy.wait()
        total = total + from_wide[k]
    o_ref[...] = total


def device_sum(x, scatter, ident):
    wide, narrow = lax.axis_size("wide"), lax.axis_size("narrow")
    middle = x.shape[1:] if scatter else x.shape
    last = middle[1:] if scatter else x.shape
    return pl.pallas_call(
        partial(sum_kernel, wide, narrow, scatter),
        out_shape=jax.ShapeDtypeStruct(last, F32),
        in_specs=[pl.BlockSpec(memory_space=pltpu.VMEM)],
        out_specs=pl.BlockSpec(memory_space=pltpu.VMEM),
        scratch_shapes=[
            pltpu.VMEM((narrow - 1,) + middle, F32),
            pltpu.VMEM(middle, F32),
            pltpu.VMEM((wide - 1,) + last, F32),
            pltpu.SemaphoreType.DMA((narrow - 1,)),
            pltpu.SemaphoreType.DMA((narrow - 1,)),
            pltpu.SemaphoreType.DMA((wide - 1,)),
            pltpu.SemaphoreType.DMA((wide - 1,)),
        ],
        compiler_params=pltpu.CompilerParams(
            collective_id=ident, has_side_effects=True, vmem_limit_bytes=LIMIT
        ),
    )(x)


def local_call(body, args, outs, scratch, smem=()):
    return pl.pallas_call(
        body,
        out_shape=[jax.ShapeDtypeStruct(s, F32) for s in outs],
        in_specs=[
            pl.BlockSpec(memory_space=pltpu.SMEM if p in smem else pltpu.VMEM)
            for p in range(len(args))
        ],
        out_specs=[pl.BlockSpec(memory_space=pltpu.VMEM)] * len(outs),
        scratch_shapes=[pltpu.VMEM(s, F32) for s in scratch],
        compiler_params=pltpu.CompilerParams(vmem_limit_bytes=LIMIT),
    )(*args)


def swap(axis, to_prev, to_next):
    count = lax.axis_size(axis)
    from_prev = lax.ppermute(to_next, axis, [(i, (i + 1) % count) for i in range(count)])
    from_next = lax.ppermute(to_prev, axis, [((i + 1) % count, i) for i in range(count)])
    return from_prev, from_next


def exchange(x, wide=False):
    width = 2 if wide else 1
    below, above = swap("wide", x[0:width], x[8 - width : 8])
    depth = 10 if wide else 8
    y, low, high = local_call(
        partial(join_kernel, wide),
        (x, below, above),
        [(depth, 64, x.shape[2]), (depth, 8, 128), (depth, 8, 128)],
        [],
    )
    return (y,) + swap("narrow", low, high)


def shards(
    velocity,
    element_slot,
    corner_vertex,
    axial_size,
    arc_size,
    radial_size,
    fdm_vectors,
    fdm_values,
):
    wide_count, narrow_count = lax.axis_size("wide"), lax.axis_size("narrow")
    er = jnp.arange(128) % RADIAL
    hz = jnp.broadcast_to(axial_size, (128,))
    ht = jnp.tile(arc_size, AROUND_DEV)
    hr = jnp.tile(radial_size, AROUND_DEV)
    volume = hz * ht * hr / 8.0
    zero = jnp.zeros((128,), F32)
    rows = [2.0 / hz, 2.0 / ht, 2.0 / hr, volume]
    rows += [jnp.where(er > 0, 1.0, 0.0), jnp.where(er < RADIAL - 1, 1.0, 0.0), zero, zero]
    geo = jnp.tile(jnp.stack(rows).astype(F32), (1, 3))
    fwd, back, stiff = jnp.asarray(FORWARD), jnp.asarray(BACKWARD), jnp.asarray(STIFF)
    wjk = jnp.broadcast_to(jnp.asarray(WEIGHT_JK)[:, None], (64, 384))
    consts = (geo, fwd, back, stiff, wjk)

    transform = fdm_vectors.T.reshape(10, 1, 10, 1) * fdm_vectors.T.reshape(1, 10, 1, 10)
    own = transform[..., 1:9].reshape(100, 80)
    blank = jnp.zeros((10, 10, 10), F32)
    halo = [blank, transform[..., 9]] + [blank] * 4 + [transform[..., 0], blank]
    halo = jnp.stack(halo, axis=-1)
    into = jnp.pad(jnp.concatenate([own, halo.reshape(100, 80)], axis=1), ((0, 12), (0, 0)))
    inner = fdm_vectors[1:9]
    outof = (inner.reshape(8, 1, 10, 1) * inner.reshape(1, 8, 1, 10)).reshape(64, 100)
    outof = jnp.pad(outof, ((0, 0), (0, 12)))
    lam2 = jnp.stack([jnp.repeat(fdm_values, 10), jnp.tile(fdm_values, 10)], axis=1)
    lam2 = jnp.pad(lam2, ((0, 12), (0, 126)), constant_values=1.0)

    mass = (np.kron(WGLL, np.kron(WGLL, WGLL)).astype(np.float32))[:, None] * volume[None]
    (field,) = local_call(enter_kernel, (velocity, element_slot, mass), [(512, 512)], [])
    field = field.reshape(8, 64, 512)

    shape = (8, 64, 384)
    u, res = local_call(first_kernel, exchange(field) + consts, [shape, shape], [(12, 64, 384)])
    for step in range(STEPS):
        total, corr = local_call(
            solve_kernel,
            exchange(res, True) + (geo, fdm_vectors, fdm_values, into, outof, lam2),
            [shape, shape],
            [(10, 112, 384), (10, 64, 384)],
            smem=(4, 5),
        )
        dirn, sums = local_call(
            direction_kernel, exchange(corr) + (total, geo, stiff, wjk), [shape, (8, 128)], []
        )
        sums = device_sum(sums, False, step)
        u, res = local_call(
            next_kernel, (u, dirn, sums) + consts, [shape, shape], [(12, 64, 384)]
        )
    owners = wide_count * narrow_count
    share = AROUND_DEV * (RADIAL + 1)
    out, full = local_call(
        partial(leave_kernel, owners),
        (u.reshape(512, 384), res.reshape(512, 384), element_slot, corner_vertex, jnp.asarray(LINEAR_JK)),
        [(3, 512, 128), (3 * owners, 256)],
        [],
    )
    blocks = full.reshape(3, wide_count, narrow_count, 256).transpose(2, 1, 0, 3)
    blocks = jnp.pad(blocks, ((0, 0), (0, 0), (0, 5), (0, 0)))
    coarse = device_sum(blocks, True, STEPS)[0:3, 0:share]
    return out, coarse


def solution(mesh):
    return jax.shard_map(
        shards,
        mesh=mesh,
        in_specs=(
            P(None, None, ("wide", "narrow")),
            P(("wide", "narrow"), None),
            P(None, ("wide", "narrow")),
            P("wide"),
            P(),
            P(),
            P(),
            P(),
        ),
        out_specs=(P(None, None, ("wide", "narrow")), P(None, ("wide", "narrow"))),
        check_vma=False,
    )
```
